32 devices in a mesh: blk: 8 (over z, core), user: 4 (over y, x).
Axes of the slice: x: 2, y: 2, z: 4, core: 2. Of those that a mesh axis runs over, the one named last changes fastest.
Arguments:
- user_factors: float32 [131072, 256], P(('blk', 'user')), may hold values from -2 to 2
- item_factors: float32 [8192, 256], P(('blk', 'user')), may hold values from -2 to 2
- block_index: int32 [3, 256, 2, 4], P(None, ('blk', 'user')), may hold values from 0 to 15, as said below
- block_count: int32 [3, 256, 2], P(None, ('blk', 'user')), may hold values from 1 to 4
- ratings: int32 [3, 256, 2, 4, 128, 128], P(None, ('blk', 'user')), may hold values from 0 to 10
Outputs:
- users_out: float32 [131072, 256], P(('blk', 'user'))
- items_out: float32 [8192, 256], P(('blk', 'user'))
The draws below stay inside these ranges and needn't reach their ends.
Inputs may be any that keep to these rules, and one draw needn't show every extreme that they name: `block_index`: the 4 block numbers of one tile are distinct.
All inputs are finite; a program needn't handle non-finite values.
Results may differ from the reference program's by a relative error of at most 0.0003.
Values sent between devices are 32-bit elements; how exact they have to be, the bound alone decides.
No kernel may reach another device: no remote copies, remote signals or barrier semaphores. Data moves between devices by JAX's collectives and lax.ppermute only.
A program may use at most 128 MiB of HBM per device.

```python
import jax
import jax.numpy as jnp
from jax import lax

R = 256
BL = 128
SUB = 4
OCC = 4
TR = 8
TC = 2
STEPS = 3
TROWS = 256
USERS = 131072
ITEMS = 8192
N_BLK = 8
N_USER = 4


def draw_block_index(key, part):
    tiles = SUB * SUB
    scores = jax.random.randint(key, (STEPS, TROWS, TC, tiles), 0, 1 << 20)
    values = jnp.arange(tiles, dtype=jnp.int32)
    scores = scores * tiles + values
    first = (jnp.arange(STEPS)[:, None, None, None] == 0) & (jnp.arange(TROWS)[None, :, None, None] == 0) & (jnp.arange(TC)[None, None, :, None] == 0)
    forced = jnp.where(values == tiles - 1, -2, jnp.where(values == 0, -1, scores))
    scores = jnp.where(first, forced, scores)
    order = jnp.argsort(scores, axis=-1, stable=True)
    return order[..., :OCC].astype(jnp.int32)


def draw_block_count(key, part):
    level_key = jax.random.fold_in(key, 11)
    count_key = jax.random.fold_in(key, 23)
    level = jax.random.randint(level_key, (STEPS, TROWS, 1), 1, OCC + 1)
    counts = jax.random.randint(count_key, (STEPS, TROWS, TC), 1, level + 1)
    first = (jnp.arange(STEPS)[:, None, None] == 0) & (jnp.arange(TROWS)[None, :, None] == 0) & (jnp.arange(TC)[None, None, :] == 0)
    return jnp.where(first, OCC, counts).astype(jnp.int32)


def with_ends(array, rng, least, high):
    longest = array.shape.index(max(array.shape))
    spots = []
    for shift in (0, 1):
        where = [jax.random.randint(jax.random.fold_in(rng, axis), (), 0, length) for axis, length in enumerate(array.shape)]
        where[longest] = (where[longest] + shift) % array.shape[longest]
        spots.append(tuple(where))
    return array.at[spots[0]].set(least).at[spots[1]].set(high)


def block_levels(own_key, extent, shards, smallest, top_value):
    level, own = 1.0, jax.random.fold_in(own_key, 6)
    for axis_at, blocks in shards:
        draws = jnp.exp(jax.random.uniform(jax.random.fold_in(own, axis_at), (blocks,), jnp.float32, smallest / len(shards), top_value / len(shards)))
        level = level * jnp.repeat(draws, extent[axis_at] // blocks).reshape([-1 if axis == axis_at else 1 for axis in range(len(extent))])
    return level


def gaussian(stream_key, shape, deviation, most, split=(), kind=jnp.bfloat16):
    entries = deviation * jax.random.normal(stream_key, shape, jnp.float32)
    if split:
        entries = entries * block_levels(stream_key, shape, split, -0.22, 0.18)
    return jnp.clip(entries, -most, most).astype(kind)


def setup_inputs(seed: int = 0) -> dict:
    key_list = jax.random.split(jax.random.key(seed), 6)
    return {
        "user_factors": gaussian(key_list[0], (USERS, R), 0.3, 2.0, ((0, 32),), jnp.float32),
        "item_factors": gaussian(key_list[1], (ITEMS, R), 0.3, 2.0, ((0, 32),), jnp.float32),
        "block_index": draw_block_index(jax.random.fold_in(key_list[5], 71), 0),
        "block_count": draw_block_count(jax.random.fold_in(key_list[5], 71), 0),
        "ratings": with_ends(jax.random.randint(key_list[4], (STEPS, TROWS, TC, OCC, BL, BL), 0, 11), jax.random.fold_in(key_list[4], 1), 0, 10).astype(jnp.int32),
    }


user_rate = 0.01
item_rate = 0.0015
decay_rate = 0.05


def local_grads(user_rows, item_group, tile_index, tile_count, tile_ratings):
    tile_rows = tile_index.shape[0]
    tile_cols = tile_index.shape[1]
    slots = tile_index.shape[2]
    rank = user_rows.shape[1]
    block = tile_ratings.shape[-1]
    parts = user_rows.shape[0] // (tile_rows * block)
    sub_row = tile_index // parts
    sub_col = tile_index % parts
    user_tiles = user_rows.reshape(tile_rows, parts, block, rank)
    item_tiles = item_group.reshape(tile_cols, parts, block, rank)
    row_ids = jnp.arange(tile_rows)[:, None, None]
    col_ids = jnp.arange(tile_cols)[None, :, None]
    user_blocks = user_tiles[row_ids, sub_row]
    item_blocks = item_tiles[col_ids, sub_col]
    predicted = jnp.einsum('abkir,abkjr->abkij', user_blocks, item_blocks, precision=lax.Precision.HIGHEST)
    slot_ids = jnp.arange(slots)[None, None, :, None, None]
    observed = (tile_ratings > 0) & (slot_ids < tile_count[:, :, None, None, None])
    residuals = jnp.where(observed, 0.5 * tile_ratings.astype(jnp.float32) - predicted, 0.0)
    user_terms = jnp.einsum('abkij,abkjr->abkir', residuals, item_blocks, precision=lax.Precision.HIGHEST)
    item_terms = jnp.einsum('abkij,abkir->abkjr', residuals, user_blocks, precision=lax.Precision.HIGHEST)
    part_ids = jnp.arange(parts)
    row_hot = (sub_row[..., None] == part_ids).astype(jnp.float32)
    col_hot = (sub_col[..., None] == part_ids).astype(jnp.float32)
    grad_users = jnp.einsum('abko,abkir->aoir', row_hot, user_terms, precision=lax.Precision.HIGHEST)
    grad_items = jnp.einsum('abko,abkjr->bojr', col_hot, item_terms, precision=lax.Precision.HIGHEST)
    return grad_users.reshape(user_rows.shape), grad_items.reshape(item_group.shape)


def reference(user_factors, item_factors, block_index, block_count, ratings):
    user_rows = user_factors
    item_rows = item_factors
    spans = N_BLK * N_USER
    group_len = TC * SUB * BL
    user_len = TR * SUB * BL
    for step in range(STEPS):
        index_step = block_index[step].reshape(spans, TR, TC, OCC)
        count_step = block_count[step].reshape(spans, TR, TC)
        rating_step = ratings[step].reshape(spans, TR, TC, OCC, BL, BL)

        def visit(grad_items, inputs):
            span, user_span, tile_index, tile_count, tile_ratings = inputs
            source = ((span // N_USER - step) % N_BLK).astype(jnp.int32)
            start = (source * group_len).astype(jnp.int32)
            item_group = lax.dynamic_slice_in_dim(item_rows, start, group_len, 0)
            grad_u, grad_v = local_grads(user_span, item_group, tile_index, tile_count, tile_ratings)
            before = lax.dynamic_slice_in_dim(grad_items, start, group_len, 0)
            grad_items = lax.dynamic_update_slice_in_dim(grad_items, before + grad_v, start, 0)
            return grad_items, grad_u

        inputs = (jnp.arange(spans, dtype=jnp.int32), user_rows.reshape(spans, user_len, R), index_step, count_step, rating_step)
        grad_items, grad_users = lax.scan(visit, jnp.zeros(item_rows.shape, jnp.float32), inputs)
        grad_users = grad_users.reshape(user_rows.shape)
        user_rows = user_rows + user_rate * (grad_users - decay_rate * user_rows)
        item_rows = item_rows + item_rate * (grad_items - decay_rate * item_rows)
    rolled = jnp.roll(item_rows.reshape(N_BLK, group_len, R), STEPS, axis=0).reshape(item_rows.shape)
    return user_rows, rolled
```

```python
import functools

import jax
import jax.numpy as jnp
from jax import lax
from jax.experimental import pallas as pl
from jax.experimental.pallas import tpu as pltpu
from jax.sharding import PartitionSpec as P

user_rate = 0.01
item_rate = 0.0015
decay_rate = 0.05
UNROLL = 2


def partner(u, r, n):
    return u ^ r if n & (n - 1) == 0 else (u + r) % n


def moved(x, step, r, nb, nu):
    route = [
        (b * nu + u, ((b + step) % nb) * nu + partner(u, r, nu))
        for b in range(nb)
        for u in range(nu)
    ]
    return lax.ppermute(x, ("blk", "user"), route)


def prep_kernel(parts, chunks, index_ref, count_ref, list_ref):
    steps, tile_rows, tile_cols, slots = index_ref.shape
    for s in range(steps):

        def tile(i, found):
            t = i // tile_cols
            c = i % tile_cols
            count = count_ref[s, t, c]
            for k in range(slots):
                q = index_ref[s, t, c, k]
                col = c * parts + q % parts
                chunk = col % chunks
                n = found[0]
                for j in range(1, chunks):
                    n = jnp.where(chunk == j, found[j], n)
                base = 4 * (s * chunks + chunk)
                list_ref[base + 1, n] = t * parts + q // parts
                list_ref[base + 2, n] = col // chunks
                list_ref[base + 3, n] = (s * tile_rows * tile_cols + i) * slots + k
                more = jnp.where(k < count, 1, 0)
                found = tuple(
                    found[j] + jnp.where(chunk == j, more, 0) for j in range(chunks)
                )
            return found

        found = lax.fori_loop(0, tile_rows * tile_cols, tile, (jnp.int32(0),) * chunks)
        for j in range(chunks):
            list_ref[4 * (s * chunks + j), 0] = found[j]


def halves(x):
    hi = x.astype(jnp.bfloat16)
    lo = (x - hi.astype(jnp.float32)).astype(jnp.bfloat16)
    return jnp.concatenate([hi, lo], axis=0)


def doubled(x):
    hi = x.astype(jnp.bfloat16)
    lo = (x - hi.astype(jnp.float32)).astype(jnp.bfloat16)
    return jnp.concatenate(
        [jnp.concatenate([hi, hi], axis=1), jnp.concatenate([lo, lo], axis=1)], axis=0
    )


def mul(a, b):
    return jnp.dot(a, b, preferred_element_type=jnp.float32)


def step_kernel(row, first, nu, *refs):
    list_ref, users, ratings = refs[:3]
    items = refs[3 : 3 + nu]
    rest = refs[3 + nu :]
    if not first:
        rest = rest[1:]
    users_next = rest[0]
    terms = rest[1 : 1 + nu]
    item_parts, item_grads = rest[1 + nu :]
    blocks, block, rank = users.shape
    me = lax.axis_index("user")
    for r in range(nu):
        item_parts[source_of(me, r, nu)] = halves(items[r][...])
    item_grads[...] = jnp.zeros_like(item_grads)
    if first:

        def scale(i, carry):
            users_next[i] = users[i] * (1.0 - user_rate * decay_rate)
            return carry

        lax.fori_loop(0, blocks, scale, 0)
    count = list_ref[4 * row, 0]

    def body(i, carry):
        done = []
        for j in range(UNROLL):
            n = i * UNROLL + j
            entry = jnp.minimum(n, count - 1)
            ub = list_ref[4 * row + 1, entry]
            ib = list_ref[4 * row + 2, entry]
            slot = list_ref[4 * row + 3, entry]
            least = jnp.where(n < count, 0, 1 << 30)
            rating = ratings[slot]
            user_part = halves(users[ub])
            item_part = item_parts[ib]
            products = lax.dot_general(
                user_part,
                item_part,
                (((1,), (1,)), ((), ())),
                preferred_element_type=jnp.float32,
            )
            predicted = (
                products[block:, block:] + products[block:, :block] + products[:block, block:]
            ) + products[:block, :block]
            residual = jnp.where(
                rating > least, 0.5 * rating.astype(jnp.float32) - predicted, 0.0
            )
            user_term = mul(doubled(residual), item_part)
            item_term = mul(doubled(residual.T), user_part)
            done.append((ub, ib, user_term, item_term))
        for ub, ib, user_term, item_term in done:
            users_next[ub] += user_rate * (user_term[:block] + user_term[block:])
            item_grads[ib] += item_term[:block] + item_term[block:]
        return carry

    lax.fori_loop(0, (count + UNROLL - 1) // UNROLL, body, 0)
    for r in range(nu):
        term = item_rate * item_grads[partner_of(me, r, nu)]
        if r == 0:
            term += items[0][...] * (1.0 - item_rate * decay_rate)
        terms[r][...] = term


def partner_of(me, r, nu):
    if r == 0:
        return me
    return me ^ r if nu & (nu - 1) == 0 else lax.rem(me + r, nu)


def source_of(me, r, nu):
    if r == 0:
        return me
    return me ^ r if nu & (nu - 1) == 0 else lax.rem(me - r + nu, nu)


def whole_in(space):
    return pl.BlockSpec(memory_space=space)


def in_vmem(x):
    return pltpu.with_memory_space_constraint(x, pltpu.VMEM)


def run_step(row, first, lists, users, users_next, ratings, items):
    nu = len(items)
    block, rank = items[0].shape
    spec = whole_in(pltpu.VMEM)
    args = [lists] + [in_vmem(x) for x in (users, ratings, *items)]
    in_specs = [whole_in(pltpu.SMEM)] + [spec] * (2 + nu)
    aliases = {}
    if not first:
        aliases = {len(args): 0}
        args.append(in_vmem(users_next))
        in_specs.append(spec)
    outs = pl.pallas_call(
        functools.partial(step_kernel, row, first, nu),
        out_shape=[pltpu.VMEM(users.shape, users.dtype)]
        + [pltpu.VMEM((block, rank), jnp.float32)] * nu,
        in_specs=in_specs,
        out_specs=[spec] * (1 + nu),
        scratch_shapes=[
            pltpu.VMEM((nu, 2 * block, rank), jnp.bfloat16),
            pltpu.VMEM((nu, block, rank), jnp.float32),
        ],
        input_output_aliases=aliases,
        compiler_params=pltpu.CompilerParams(vmem_limit_bytes=16 << 20),
    )(*args)
    return outs[0], outs[1:]


def local(nb, nu, user_factors, item_factors, block_index, block_count, ratings):
    steps, tile_rows, tile_cols, slots = block_index.shape
    block = ratings.shape[-1]
    rank = user_factors.shape[1]
    parts = user_factors.shape[0] // (tile_rows * block)
    chunks = item_factors.shape[0] // block
    total = tile_rows * tile_cols * slots
    lists = pl.pallas_call(
        functools.partial(prep_kernel, parts, chunks),
        out_shape=jax.ShapeDtypeStruct((4 * steps * chunks, total), jnp.int32),
        in_specs=[whole_in(pltpu.SMEM)] * 2,
        out_specs=whole_in(pltpu.SMEM),
    )(block_index, block_count)
    users = user_factors.reshape(-1, block, rank)
    blocks = ratings.reshape(steps * total, block, block)
    own = [item_factors[k * block : (k + 1) * block] for k in range(chunks)]
    for s in range(steps):
        users_next = None
        fresh = []
        for k in range(chunks):
            items = [moved(own[k], 0, r, nb, nu) if r else own[k] for r in range(nu)]
            users_next, terms = run_step(
                s * chunks + k, k == 0, lists, users, users_next, blocks, items
            )
            sent = [moved(terms[r], 1, r, nb, nu) for r in range(nu)]
            fresh.append(functools.reduce(jnp.add, sent))
        own = fresh
        users = users_next
    return (users.reshape(user_factors.shape), jnp.concatenate(own, axis=0))


def solution(mesh):
    in_specs = (
        P(("blk", "user"), None),
        P(("blk", "user"), None),
        P(None, ("blk", "user"), None, None),
        P(None, ("blk", "user"), None),
        P(None, ("blk", "user"), None, None, None, None),
    )
    out_specs = (P(("blk", "user"), None), P(("blk", "user"), None))
    return jax.shard_map(
        functools.partial(local, mesh.shape["blk"], mesh.shape["user"]),
        mesh=mesh,
        in_specs=in_specs,
        out_specs=out_specs,
        check_vma=False,
    )
```

```python
import functools

import jax
import jax.numpy as jnp
from jax import lax
from jax.experimental import pallas as pl
from jax.experimental.pallas import tpu as pltpu
from jax.sharding import PartitionSpec as P

user_rate = 0.01
item_rate = 0.0015
decay_rate = 0.05
GROUPS = (8, 4)


def divided(x, n):
    return x >> (n.bit_length() - 1) if n & (n - 1) == 0 else lax.div(x, n)


def left_over(x, n):
    return x & (n - 1) if n & (n - 1) == 0 else lax.rem(x, n)


def partner(u, r, n):
    return u ^ r if n & (n - 1) == 0 else (u + r) % n


def source(u, r, n):
    return u ^ r if n & (n - 1) == 0 else (u - r + n) % n


def moved(x, step, r, nb, nu):
    route = [
        (b * nu + u, ((b + step) % nb) * nu + partner(u, r, nu))
        for b in range(nb)
        for u in range(nu)
    ]
    return lax.ppermute(x, ("blk", "user"), route)


def split(x):
    hi = x.astype(jnp.bfloat16)
    return hi, (x - hi.astype(jnp.float32)).astype(jnp.bfloat16)


def dot(a, b):
    return jnp.dot(a, b, preferred_element_type=jnp.float32)


def dot_rows(a, b):
    return lax.dot_general(a, b, (((1,), (1,)), ((), ())), preferred_element_type=jnp.float32)


def dot_split(x_hi, x_lo, y_hi, y_lo):
    wide = jnp.concatenate([x_hi, x_lo], axis=1)
    return dot(wide, jnp.concatenate([y_hi, y_hi], axis=0)) + dot(x_hi, y_lo)


def over_groups(count, body):
    first = 0
    for i, size in enumerate(GROUPS):
        groups = divided(count - first + (size - 1 if i + 1 == len(GROUPS) else 0), size)

        def step(g, carry, first=first, size=size):
            body(first + g * size, size)
            return carry

        lax.fori_loop(0, groups, step, 0)
        first = first + groups * size


class Shape:
    def __init__(self, user_factors, item_factors, block_index, ratings):
        self.steps, self.tile_rows, self.tile_cols, self.slots = block_index.shape
        self.block = ratings.shape[-1]
        self.rank = user_factors.shape[1]
        self.parts = user_factors.shape[0] // (self.tile_rows * self.block)
        self.chunks = item_factors.shape[0] // self.block
        self.total = self.tile_rows * self.tile_cols * self.slots
        self.user_blocks = self.tile_rows * self.parts

    def entry(self, packed):
        q = left_over(packed, self.parts * self.parts)
        slot = divided(packed, self.parts * self.parts)
        tile = divided(slot, self.slots)
        row = divided(tile, self.tile_cols) * self.parts + divided(q, self.parts)
        col = left_over(tile, self.tile_cols) * self.parts + left_over(q, self.parts)
        return slot, row, divided(col, self.chunks)


def load_kernel(sh, index_ref, count_ref, users_in, ratings_in, users, ratings, lists, sems):
    copies = [
        pltpu.make_async_copy(users_in, users, sems.at[0]),
        pltpu.make_async_copy(ratings_in.at[pl.ds(0, sh.total)], ratings, sems.at[1]),
    ]
    for copy in copies:
        copy.start()
    for s in range(sh.steps):

        def tile_row(t, found):
            for c in range(sh.tile_cols):
                count = count_ref[s, c, t]
                for k in range(sh.slots):
                    q = index_ref[s, c, k, t]
                    chunk = left_over(q + c * sh.parts, sh.chunks)
                    n = found[0]
                    for j in range(1, sh.chunks):
                        n = jnp.where(chunk == j, found[j], n)
                    slot = (t * sh.tile_cols + c) * sh.slots + k
                    lists[s * sh.chunks + chunk, n + 1] = slot * (sh.parts * sh.parts) + q
                    more = jnp.where(k < count, 1, 0)
                    found = tuple(
                        found[j] + jnp.where(chunk == j, more, 0) for j in range(sh.chunks)
                    )
            return found

        found = lax.fori_loop(0, sh.tile_rows, tile_row, (jnp.int32(0),) * sh.chunks)
        for j in range(sh.chunks):
            lists[s * sh.chunks + j, 0] = found[j]
    for copy in copies:
        copy.wait()


def item_kernel(sh, nu, row, *refs):
    list_ref, users, ratings = refs[:3]
    items = refs[3 : 3 + nu]
    terms = refs[3 + nu : 3 + 2 * nu]
    residuals, item_parts, grads, item_turned = refs[3 + 2 * nu :]
    block = sh.block
    me = lax.axis_index("user")
    for r in range(nu):
        hi, lo = split(items[r][...])
        at = source(me, r, nu)
        item_parts[at, :block] = hi
        item_parts[at, block:] = lo
        hi, lo = split(items[r][...].T)
        item_turned[at, :, :block] = hi
        item_turned[at, :, block:] = lo
    grads[...] = jnp.zeros_like(grads)
    count = list_ref[row, 0]

    def body(first, size):
        found = []
        for n in [first + j for j in range(size)]:
            slot, ub, ib = sh.entry(list_ref[row, jnp.minimum(n, count - 1) + 1])
            found.append((n, slot, ub, ib, jnp.where(n < count, 0, 1 << 30)))
        predicted = []
        for n, slot, ub, ib, least in found:
            u_hi, u_lo = split(users[ub])
            wide = dot(u_hi, item_turned[ib])
            narrow = dot(u_lo, item_turned[ib, :, :block])
            predicted.append((wide[:, block:] + narrow) + wide[:, :block])
        kept = []
        for (n, slot, ub, ib, least), p in zip(found, predicted):
            rating = ratings[slot]
            kept.append(jnp.where(rating > least, 0.5 * rating.astype(jnp.float32) - p, 0.0))
        sums = [
            dot_split(*split(residual.T), *split(users[ub]))
            for (n, slot, ub, ib, least), residual in zip(found, kept)
        ]
        for (n, slot, ub, ib, least), term in zip(found, sums):
            grads[ib] += term
        for (n, slot, ub, ib, least), residual in zip(found, kept):
            hi, lo = split(residual)
            residuals[n, :block] = hi
            residuals[n, block:] = lo

    over_groups(count, body)
    for r in range(nu):
        term = item_rate * grads[partner(me, r, nu)]
        if r == 0:
            term += items[0][...] * (1.0 - item_rate * decay_rate)
        terms[r][...] = term


def user_kernel(sh, step, *refs):
    list_ref, users = refs[:2]
    residuals = refs[2 : 2 + sh.chunks]
    item_parts = refs[2 + sh.chunks : 2 + 2 * sh.chunks]
    row = step * sh.chunks
    if step + 1 < sh.steps:
        ratings_in, users_next, ratings, sem = refs[2 + 2 * sh.chunks :]
        copy = pltpu.make_async_copy(
            ratings_in.at[pl.ds((step + 1) * sh.total, sh.total)], ratings, sem
        )
        copy.start()
    else:
        (users_next,) = refs[2 + 2 * sh.chunks :]
    block = sh.block

    def scale(i, carry):
        users_next[i] = users[i] * (1.0 - user_rate * decay_rate)
        return carry

    lax.fori_loop(0, sh.user_blocks, scale, 0)
    for k in range(sh.chunks):
        count = list_ref[row + k, 0]

        def body(first, size, k=k, count=count):
            found = []
            for n in [first + j for j in range(size)]:
                slot, ub, ib = sh.entry(list_ref[row + k, jnp.minimum(n, count - 1) + 1])
                found.append((n, ub, ib))
            terms = []
            for n, ub, ib in found:
                hi, lo = residuals[k][n, :block], residuals[k][n, block:]
                v_hi, v_lo = item_parts[k][ib, :block], item_parts[k][ib, block:]
                terms.append(user_rate * dot_split(hi, lo, v_hi, v_lo))
            for (n, ub, ib), term in zip(found, terms):
                users_next[ub] += term

        over_groups(count, body)
    if step + 1 < sh.steps:
        copy.wait()


def whole_in(space):
    return pl.BlockSpec(memory_space=space)


def in_vmem(x):
    return pltpu.with_memory_space_constraint(x, pltpu.VMEM)


def in_hbm(x):
    return pltpu.with_memory_space_constraint(x, pltpu.HBM)


def params():
    return pltpu.CompilerParams(vmem_limit_bytes=16 << 20)


def load(sh, index, count, users, blocks):
    return pl.pallas_call(
        functools.partial(load_kernel, sh),
        out_shape=[
            pltpu.VMEM(users.shape, users.dtype),
            pltpu.VMEM((sh.total, sh.block, sh.block), blocks.dtype),
            jax.ShapeDtypeStruct((sh.steps * sh.chunks, sh.total + 1), jnp.int32),
        ],
        in_specs=[whole_in(pltpu.SMEM)] * 2 + [whole_in(pl.ANY)] * 2,
        out_specs=[whole_in(pltpu.VMEM)] * 2 + [whole_in(pltpu.SMEM)],
        scratch_shapes=[pltpu.SemaphoreType.DMA((2,))],
        compiler_params=params(),
    )(*[in_hbm(x) for x in (index, count, users, blocks)])


def item_terms(sh, row, lists, users, ratings, items):
    nu = len(items)
    spec = whole_in(pltpu.VMEM)
    padded = -(-sh.total // GROUPS[0]) * GROUPS[0]
    outs = pl.pallas_call(
        functools.partial(item_kernel, sh, nu, row),
        out_shape=[pltpu.VMEM((sh.block, sh.rank), jnp.float32)] * nu
        + [
            pltpu.VMEM((padded, 2 * sh.block, sh.block), jnp.bfloat16),
            pltpu.VMEM((nu, 2 * sh.block, sh.rank), jnp.bfloat16),
        ],
        in_specs=[whole_in(pltpu.SMEM)] + [spec] * (2 + nu),
        out_specs=[spec] * (2 + nu),
        scratch_shapes=[
            pltpu.VMEM((nu, sh.block, sh.rank), jnp.float32),
            pltpu.VMEM((nu, sh.rank, 2 * sh.block), jnp.bfloat16),
        ],
        compiler_params=params(),
        cost_estimate=pl.CostEstimate(
            flops=sh.total * 8 * sh.block * sh.block * sh.rank // sh.chunks,
            bytes_accessed=8 * sh.total * sh.block * sh.block // sh.chunks,
            transcendentals=0,
        ),
    )(lists, *[in_vmem(x) for x in (users, ratings, *items)])
    return outs[:nu], outs[nu], outs[nu + 1]


def new_users(sh, step, lists, users, residuals, item_parts, blocks):
    spec = whole_in(pltpu.VMEM)
    more = step + 1 < sh.steps
    work = sh.total * 8 * sh.block * sh.block * sh.rank
    size = sh.block * sh.block
    out = pl.pallas_call(
        functools.partial(user_kernel, sh, step),
        out_shape=[pltpu.VMEM(users.shape, users.dtype)]
        + [pltpu.VMEM((sh.total, sh.block, sh.block), blocks.dtype)] * more,
        in_specs=[whole_in(pltpu.SMEM)]
        + [spec] * (1 + 2 * sh.chunks)
        + [whole_in(pl.ANY)] * more,
        out_specs=[spec] * (1 + more),
        scratch_shapes=[pltpu.SemaphoreType.DMA] * more,
        compiler_params=params(),
        cost_estimate=pl.CostEstimate(
            flops=work, bytes_accessed=8 * users.size + 8 * sh.total * size, transcendentals=0
        ),
    )(
        lists,
        *[in_vmem(x) for x in (users, *residuals, *item_parts)],
        *[in_hbm(blocks)] * more,
    )
    return out[0], out[1] if more else None


def local(nb, nu, user_factors, item_factors, block_index, block_count, ratings):
    sh = Shape(user_factors, item_factors, block_index, ratings)
    index = block_index.transpose(0, 2, 3, 1)
    count = block_count.transpose(0, 2, 1)
    users = user_factors.reshape(-1, sh.block, sh.rank)
    blocks = ratings.reshape(-1, sh.block, sh.block)
    own = [item_factors[k * sh.block : (k + 1) * sh.block] for k in range(sh.chunks)]
    users, step_ratings, lists = load(sh, index, count, users, blocks)
    for s in range(sh.steps):
        sent, residuals, item_parts = [], [], []
        for k in range(sh.chunks):
            items = [moved(own[k], 0, r, nb, nu) if r else own[k] for r in range(nu)]
            terms, residual, parts = item_terms(
                sh, s * sh.chunks + k, lists, users, step_ratings, items
            )
            residuals.append(residual)
            item_parts.append(parts)
            sent.append([moved(terms[r], 1, r, nb, nu) for r in range(nu)])
        own = [functools.reduce(jnp.add, x) for x in sent[:-1]]
        own, residuals = lax.optimization_barrier((own, residuals))
        users, step_ratings = new_users(
            sh, s, lists, users, residuals, item_parts, blocks
        )
        sent, users = lax.optimization_barrier((sent[-1], users))
        own.append(functools.reduce(jnp.add, sent))
    return (users.reshape(user_factors.shape), jnp.concatenate(own, axis=0))


def solution(mesh):
    in_specs = (
        P(("blk", "user"), None),
        P(("blk", "user"), None),
        P(None, ("blk", "user"), None, None),
        P(None, ("blk", "user"), None),
        P(None, ("blk", "user"), None, None, None, None),
    )
    out_specs = (P(("blk", "user"), None), P(("blk", "user"), None))
    return jax.shard_map(
        functools.partial(local, mesh.shape["blk"], mesh.shape["user"]),
        mesh=mesh,
        in_specs=in_specs,
        out_specs=out_specs,
        check_vma=False,
    )
```

```python
import functools

import jax
import jax.numpy as jnp
from jax import lax
from jax.experimental import pallas as pl
from jax.experimental.pallas import tpu as pltpu
from jax.sharding import PartitionSpec as P

user_rate = 0.01
item_rate = 0.0015
decay_rate = 0.05
GROUPS = (8, 4)


def divided(x, n):
    return x >> (n.bit_length() - 1) if n & (n - 1) == 0 else lax.div(x, n)


def left_over(x, n):
    return x & (n - 1) if n & (n - 1) == 0 else lax.rem(x, n)


def partner(u, r, n):
    return u ^ r if n & (n - 1) == 0 else (u + r) % n


def source(u, r, n):
    return u ^ r if n & (n - 1) == 0 else (u - r + n) % n


def moved(x, step, r, nb, nu):
    route = [
        (b * nu + u, ((b + step) % nb) * nu + partner(u, r, nu))
        for b in range(nb)
        for u in range(nu)
    ]
    return lax.ppermute(x, ("blk", "user"), route)


def split(x):
    hi = x.astype(jnp.bfloat16)
    return hi, (x - hi.astype(jnp.float32)).astype(jnp.bfloat16)


def dot(a, b):
    return jnp.dot(a, b, preferred_element_type=jnp.float32)


def dot_rows(a, b):
    return lax.dot_general(a, b, (((1,), (1,)), ((), ())), preferred_element_type=jnp.float32)


def dot_split(x_hi, x_lo, y_hi, y_lo):
    wide = jnp.concatenate([x_hi, x_lo], axis=1)
    return dot(wide, jnp.concatenate([y_hi, y_hi], axis=0)) + dot(x_hi, y_lo)


def over_groups(count, body):
    first = 0
    for i, size in enumerate(GROUPS):
        groups = divided(count - first + (size - 1 if i + 1 == len(GROUPS) else 0), size)

        def step(g, carry, first=first, size=size):
            body(first + g * size, size)
            return carry

        lax.fori_loop(0, groups, step, 0)
        first = first + groups * size


class Shape:
    def __init__(self, user_factors, item_factors, block_index, ratings):
        self.steps, self.tile_rows, self.tile_cols, self.slots = block_index.shape
        self.block = ratings.shape[-1]
        self.rank = user_factors.shape[1]
        self.parts = user_factors.shape[0] // (self.tile_rows * self.block)
        self.chunks = item_factors.shape[0] // self.block
        self.total = self.tile_rows * self.tile_cols * self.slots
        self.user_blocks = self.tile_rows * self.parts

    def entry(self, packed):
        q = left_over(packed, self.parts * self.parts)
        slot = divided(packed, self.parts * self.parts)
        tile = divided(slot, self.slots)
        row = divided(tile, self.tile_cols) * self.parts + divided(q, self.parts)
        col = left_over(tile, self.tile_cols) * self.parts + left_over(q, self.parts)
        return slot, row, divided(col, self.chunks)


def load_kernel(sh, index_ref, count_ref, users_in, ratings_in, users, ratings, lists, sems):
    copies = [
        pltpu.make_async_copy(users_in, users, sems.at[0]),
        pltpu.make_async_copy(ratings_in.at[pl.ds(0, sh.total)], ratings, sems.at[1]),
    ]
    for copy in copies:
        copy.start()
    for s in range(sh.steps):

        def tile_row(t, found):
            for c in range(sh.tile_cols):
                count = count_ref[s, c, t]
                for k in range(sh.slots):
                    q = index_ref[s, c, k, t]
                    chunk = left_over(q + c * sh.parts, sh.chunks)
                    n = found[0]
                    for j in range(1, sh.chunks):
                        n = jnp.where(chunk == j, found[j], n)
                    slot = (t * sh.tile_cols + c) * sh.slots + k
                    lists[s * sh.chunks + chunk, n + 1] = slot * (sh.parts * sh.parts) + q
                    more = jnp.where(k < count, 1, 0)
                    found = tuple(
                        found[j] + jnp.where(chunk == j, more, 0) for j in range(sh.chunks)
                    )
            return found

        found = lax.fori_loop(0, sh.tile_rows, tile_row, (jnp.int32(0),) * sh.chunks)
        for j in range(sh.chunks):
            lists[s * sh.chunks + j, 0] = found[j]
    for copy in copies:
        copy.wait()


def item_kernel(sh, nu, row, *refs):
    list_ref, users, ratings = refs[:3]
    items = refs[3 : 3 + nu]
    terms = refs[3 + nu : 3 + 2 * nu]
    residuals, item_parts, grads, item_turned = refs[3 + 2 * nu :]
    block = sh.block
    me = lax.axis_index("user")
    for r in range(nu):
        hi, lo = split(items[r][...])
        at = source(me, r, nu)
        item_parts[at, :block] = hi
        item_parts[at, block:] = lo
        hi, lo = split(items[r][...].T)
        item_turned[at, :, :block] = hi
        item_turned[at, :, block:] = lo
    grads[...] = jnp.zeros_like(grads)
    count = list_ref[row, 0]

    def body(first, size):
        found = []
        for n in [first + j for j in range(size)]:
            slot, ub, ib = sh.entry(list_ref[row, jnp.minimum(n, count - 1) + 1])
            found.append((n, slot, ub, ib, jnp.where(n < count, 0, 1 << 30)))
        predicted = []
        for n, slot, ub, ib, least in found:
            u_hi, u_lo = split(users[ub])
            wide = dot(u_hi, item_turned[ib])
            narrow = dot(u_lo, item_turned[ib, :, :block])
            predicted.append((wide[:, block:] + narrow) + wide[:, :block])
        kept = []
        for (n, slot, ub, ib, least), p in zip(found, predicted):
            rating = ratings[slot]
            kept.append(jnp.where(rating > least, 0.5 * rating.astype(jnp.float32) - p, 0.0))
        sums = [
            dot_split(*split(residual.T), *split(users[ub]))
            for (n, slot, ub, ib, least), residual in zip(found, kept)
        ]
        for (n, slot, ub, ib, least), term in zip(found, sums):
            grads[ib] += term
        for (n, slot, ub, ib, least), residual in zip(found, kept):
            hi, lo = split(residual)
            residuals[n, :block] = hi
            residuals[n, block:] = lo

    over_groups(count, body)
    for r in range(nu):
        term = item_rate * grads[partner(me, r, nu)]
        if r == 0:
            term += items[0][...] * (1.0 - item_rate * decay_rate)
        terms[r][...] = term


def user_kernel(sh, step, *refs):
    list_ref, users = refs[:2]
    residuals = refs[2 : 2 + sh.chunks]
    item_parts = refs[2 + sh.chunks : 2 + 2 * sh.chunks]
    row = step * sh.chunks
    if step + 1 < sh.steps:
        ratings_in, users_next, ratings, sem = refs[2 + 2 * sh.chunks :]
        copy = pltpu.make_async_copy(
            ratings_in.at[pl.ds((step + 1) * sh.total, sh.total)], ratings, sem
        )
        copy.start()
    else:
        users_out, users_next, sem = refs[2 + 2 * sh.chunks :]
    block = sh.block

    def scale(i, carry):
        users_next[i] = users[i] * (1.0 - user_rate * decay_rate)
        return carry

    lax.fori_loop(0, sh.user_blocks, scale, 0)
    for k in range(sh.chunks):
        count = list_ref[row + k, 0]

        def body(first, size, k=k, count=count):
            found = []
            for n in [first + j for j in range(size)]:
                slot, ub, ib = sh.entry(list_ref[row + k, jnp.minimum(n, count - 1) + 1])
                found.append((n, ub, ib))
            terms = []
            for n, ub, ib in found:
                hi, lo = residuals[k][n, :block], residuals[k][n, block:]
                v_hi, v_lo = item_parts[k][ib, :block], item_parts[k][ib, block:]
                terms.append(user_rate * dot_split(hi, lo, v_hi, v_lo))
            for (n, ub, ib), term in zip(found, terms):
                users_next[ub] += term

        over_groups(count, body)
    if step + 1 == sh.steps:
        copy = pltpu.make_async_copy(users_next, users_out, sem)
        copy.start()
    copy.wait()


def whole_in(space):
    return pl.BlockSpec(memory_space=space)


def in_vmem(x):
    return pltpu.with_memory_space_constraint(x, pltpu.VMEM)


def in_hbm(x):
    return pltpu.with_memory_space_constraint(x, pltpu.HBM)


def params():
    return pltpu.CompilerParams(vmem_limit_bytes=16 << 20)


def load(sh, index, count, users, blocks):
    return pl.pallas_call(
        functools.partial(load_kernel, sh),
        out_shape=[
            pltpu.VMEM(users.shape, users.dtype),
            pltpu.VMEM((sh.total, sh.block, sh.block), blocks.dtype),
            jax.ShapeDtypeStruct((sh.steps * sh.chunks, sh.total + 1), jnp.int32),
        ],
        in_specs=[whole_in(pltpu.SMEM)] * 2 + [whole_in(pl.ANY)] * 2,
        out_specs=[whole_in(pltpu.VMEM)] * 2 + [whole_in(pltpu.SMEM)],
        scratch_shapes=[pltpu.SemaphoreType.DMA((2,))],
        compiler_params=params(),
    )(*[in_hbm(x) for x in (index, count, users, blocks)])


def item_terms(sh, row, lists, users, ratings, items):
    nu = len(items)
    spec = whole_in(pltpu.VMEM)
    padded = -(-sh.total // GROUPS[0]) * GROUPS[0]
    outs = pl.pallas_call(
        functools.partial(item_kernel, sh, nu, row),
        out_shape=[pltpu.VMEM((sh.block, sh.rank), jnp.float32)] * nu
        + [
            pltpu.VMEM((padded, 2 * sh.block, sh.block), jnp.bfloat16),
            pltpu.VMEM((nu, 2 * sh.block, sh.rank), jnp.bfloat16),
        ],
        in_specs=[whole_in(pltpu.SMEM)] + [spec] * (2 + nu),
        out_specs=[spec] * (2 + nu),
        scratch_shapes=[
            pltpu.VMEM((nu, sh.block, sh.rank), jnp.float32),
            pltpu.VMEM((nu, sh.rank, 2 * sh.block), jnp.bfloat16),
        ],
        compiler_params=params(),
        cost_estimate=pl.CostEstimate(
            flops=sh.total * 8 * sh.block * sh.block * sh.rank // sh.chunks,
            bytes_accessed=8 * sh.total * sh.block * sh.block // sh.chunks,
            transcendentals=0,
        ),
    )(lists, *[in_vmem(x) for x in (users, ratings, *items)])
    return outs[:nu], outs[nu], outs[nu + 1]


def new_users(sh, step, lists, users, residuals, item_parts, blocks):
    spec = whole_in(pltpu.VMEM)
    more = step + 1 < sh.steps
    work = sh.total * 8 * sh.block * sh.block * sh.rank
    size = sh.block * sh.block
    if more:
        out_shape = [
            pltpu.VMEM(users.shape, users.dtype),
            pltpu.VMEM((sh.total, sh.block, sh.block), blocks.dtype),
        ]
        out_specs = [spec, spec]
        scratch = []
    else:
        out_shape = [jax.ShapeDtypeStruct(users.shape, users.dtype)]
        out_specs = [whole_in(pl.ANY)]
        scratch = [pltpu.VMEM(users.shape, users.dtype)]
    out = pl.pallas_call(
        functools.partial(user_kernel, sh, step),
        out_shape=out_shape,
        in_specs=[whole_in(pltpu.SMEM)]
        + [spec] * (1 + 2 * sh.chunks)
        + [whole_in(pl.ANY)] * more,
        out_specs=out_specs,
        scratch_shapes=scratch + [pltpu.SemaphoreType.DMA],
        compiler_params=params(),
        cost_estimate=pl.CostEstimate(
            flops=work, bytes_accessed=8 * users.size + 8 * sh.total * size, transcendentals=0
        ),
    )(
        lists,
        *[in_vmem(x) for x in (users, *residuals, *item_parts)],
        *[in_hbm(blocks)] * more,
    )
    return out[0], out[1] if more else None


def local(nb, nu, user_factors, item_factors, block_index, block_count, ratings):
    sh = Shape(user_factors, item_factors, block_index, ratings)
    index = block_index.transpose(0, 2, 3, 1)
    count = block_count.transpose(0, 2, 1)
    users = user_factors.reshape(-1, sh.block, sh.rank)
    blocks = ratings.reshape(-1, sh.block, sh.block)
    own = [item_factors[k * sh.block : (k + 1) * sh.block] for k in range(sh.chunks)]
    users, step_ratings, lists = load(sh, index, count, users, blocks)
    for s in range(sh.steps):
        sent, residuals, item_parts = [], [], []
        for k in range(sh.chunks):
            items = [moved(own[k], 0, r, nb, nu) if r else own[k] for r in range(nu)]
            terms, residual, parts = item_terms(
                sh, s * sh.chunks + k, lists, users, step_ratings, items
            )
            residuals.append(residual)
            item_parts.append(parts)
            sent.append([moved(terms[r], 1, r, nb, nu) for r in reversed(range(nu))])
        own = [functools.reduce(jnp.add, x) for x in sent[:-1]]
        own, residuals = lax.optimization_barrier((own, residuals))
        users, step_ratings = new_users(
            sh, s, lists, users, residuals, item_parts, blocks
        )
        sent, users = lax.optimization_barrier((sent[-1], users))
        own.append(functools.reduce(jnp.add, sent))
    return (users.reshape(user_factors.shape), jnp.concatenate(own, axis=0))


def solution(mesh):
    in_specs = (
        P(("blk", "user"), None),
        P(("blk", "user"), None),
        P(None, ("blk", "user"), None, None),
        P(None, ("blk", "user"), None),
        P(None, ("blk", "user"), None, None, None, None),
    )
    out_specs = (P(("blk", "user"), None), P(("blk", "user"), None))
    return jax.shard_map(
        functools.partial(local, mesh.shape["blk"], mesh.shape["user"]),
        mesh=mesh,
        in_specs=in_specs,
        out_specs=out_specs,
        check_vma=False,
    )
```

```python
import functools

import jax
import jax.numpy as jnp
from jax import lax
from jax.experimental import pallas as pl
from jax.experimental.pallas import tpu as pltpu
from jax.sharding import PartitionSpec as P

user_rate = 0.01
item_rate = 0.0015
decay_rate = 0.05
GROUPS = (8, 4)


def divided(x, n):
    return x >> (n.bit_length() - 1) if n & (n - 1) == 0 else lax.div(x, n)


def left_over(x, n):
    return x & (n - 1) if n & (n - 1) == 0 else lax.rem(x, n)


def partner(u, r, n):
    return u ^ r if n & (n - 1) == 0 else (u + r) % n


def source(u, r, n):
    return u ^ r if n & (n - 1) == 0 else (u - r + n) % n


def moved(x, step, r, nb, nu):
    route = [
        (b * nu + u, ((b + step) % nb) * nu + partner(u, r, nu))
        for b in range(nb)
        for u in range(nu)
    ]
    return lax.ppermute(x, ("blk", "user"), route)


def split(x):
    hi = x.astype(jnp.bfloat16)
    return hi, (x - hi.astype(jnp.float32)).astype(jnp.bfloat16)


def dot(a, b):
    return jnp.dot(a, b, preferred_element_type=jnp.float32)


def dot_rows(a, b):
    return lax.dot_general(a, b, (((1,), (1,)), ((), ())), preferred_element_type=jnp.float32)


def dot_split(x_hi, x_lo, y_hi, y_lo):
    wide = jnp.concatenate([x_hi, x_lo], axis=1)
    return dot(wide, jnp.concatenate([y_hi, y_hi], axis=0)) + dot(x_hi, y_lo)


def over_groups(count, body):
    first = 0
    for i, size in enumerate(GROUPS):
        groups = divided(count - first + (size - 1 if i + 1 == len(GROUPS) else 0), size)

        def step(g, carry, first=first, size=size):
            body(first + g * size, size)
            return carry

        lax.fori_loop(0, groups, step, 0)
        first = first + groups * size


class Shape:
    def __init__(self, user_factors, item_factors, block_index, ratings):
        self.steps, self.tile_rows, self.tile_cols, self.slots = block_index.shape
        self.block = ratings.shape[-1]
        self.rank = user_factors.shape[1]
        self.parts = user_factors.shape[0] // (self.tile_rows * self.block)
        self.chunks = item_factors.shape[0] // self.block
        self.total = self.tile_rows * self.tile_cols * self.slots
        self.user_blocks = self.tile_rows * self.parts

    def entry(self, packed):
        q = left_over(packed, self.parts * self.parts)
        slot = divided(packed, self.parts * self.parts)
        tile = divided(slot, self.slots)
        row = divided(tile, self.tile_cols) * self.parts + divided(q, self.parts)
        col = left_over(tile, self.tile_cols) * self.parts + left_over(q, self.parts)
        return slot, row, divided(col, self.chunks)


def load_kernel(sh, index_ref, count_ref, users_in, ratings_in, users, ratings, lists, sems):
    copies = [
        pltpu.make_async_copy(users_in, users, sems.at[0]),
        pltpu.make_async_copy(ratings_in.at[pl.ds(0, sh.total)], ratings, sems.at[1]),
    ]
    for copy in copies:
        copy.start()
    for s in range(sh.steps):

        def tile_row(t, found):
            for c in range(sh.tile_cols):
                count = count_ref[s, c, t]
                for k in range(sh.slots):
                    q = index_ref[s, c, k, t]
                    chunk = left_over(q + c * sh.parts, sh.chunks)
                    n = found[0]
                    for j in range(1, sh.chunks):
                        n = jnp.where(chunk == j, found[j], n)
                    slot = (t * sh.tile_cols + c) * sh.slots + k
                    lists[s * sh.chunks + chunk, n + 1] = slot * (sh.parts * sh.parts) + q
                    more = jnp.where(k < count, 1, 0)
                    found = tuple(
                        found[j] + jnp.where(chunk == j, more, 0) for j in range(sh.chunks)
                    )
            return found

        found = lax.fori_loop(0, sh.tile_rows, tile_row, (jnp.int32(0),) * sh.chunks)
        for j in range(sh.chunks):
            lists[s * sh.chunks + j, 0] = found[j]
    for copy in copies:
        copy.wait()


def item_kernel(sh, nu, row, *refs):
    list_ref, users, ratings = refs[:3]
    items = refs[3 : 3 + nu]
    terms = refs[3 + nu : 3 + 2 * nu]
    residuals, item_parts, grads, item_turned = refs[3 + 2 * nu :]
    block = sh.block
    me = lax.axis_index("user")
    for r in range(nu):
        hi, lo = split(items[r][...])
        at = source(me, r, nu)
        item_parts[at, :block] = hi
        item_parts[at, block:] = lo
        hi, lo = split(items[r][...].T)
        item_turned[at, :, :block] = hi
        item_turned[at, :, block:] = lo
    grads[...] = jnp.zeros_like(grads)
    count = list_ref[row, 0]

    def body(first, size):
        found = []
        for n in [first + j for j in range(size)]:
            slot, ub, ib = sh.entry(list_ref[row, jnp.minimum(n, count - 1) + 1])
            found.append((n, slot, ub, ib, jnp.where(n < count, 0, 1 << 30)))
        predicted = []
        for n, slot, ub, ib, least in found:
            u_hi, u_lo = split(users[ub])
            wide = dot(u_hi, item_turned[ib])
            narrow = dot(u_lo, item_turned[ib, :, :block])
            predicted.append((wide[:, block:] + narrow) + wide[:, :block])
        kept = []
        for (n, slot, ub, ib, least), p in zip(found, predicted):
            rating = ratings[slot]
            kept.append(jnp.where(rating > least, 0.5 * rating.astype(jnp.float32) - p, 0.0))
        sums = [
            dot_split(*split(residual.T), *split(users[ub]))
            for (n, slot, ub, ib, least), residual in zip(found, kept)
        ]
        for (n, slot, ub, ib, least), term in zip(found, sums):
            grads[ib] += term
        for (n, slot, ub, ib, least), residual in zip(found, kept):
            hi, lo = split(residual)
            residuals[n, :block] = hi
            residuals[n, block:] = lo

    over_groups(count, body)
    for r in range(nu):
        term = item_rate * grads[partner(me, r, nu)]
        if r == 0:
            term += items[0][...] * (1.0 - item_rate * decay_rate)
        terms[r][...] = term


def user_kernel(sh, step, *refs):
    list_ref, users = refs[:2]
    residuals = refs[2 : 2 + sh.chunks]
    item_parts = refs[2 + sh.chunks : 2 + 2 * sh.chunks]
    row = step * sh.chunks
    if step + 1 < sh.steps:
        ratings_in, users_next, ratings, sem = refs[2 + 2 * sh.chunks :]
        copy = pltpu.make_async_copy(
            ratings_in.at[pl.ds((step + 1) * sh.total, sh.total)], ratings, sem
        )
        copy.start()
    else:
        users_out, users_next, sem = refs[2 + 2 * sh.chunks :]
    block = sh.block

    def scale(i, carry):
        users_next[i] = users[i] * (1.0 - user_rate * decay_rate)
        return carry

    lax.fori_loop(0, sh.user_blocks, scale, 0)
    for k in range(sh.chunks):
        count = list_ref[row + k, 0]

        def body(first, size, k=k, count=count):
            found = []
            for n in [first + j for j in range(size)]:
                slot, ub, ib = sh.entry(list_ref[row + k, jnp.minimum(n, count - 1) + 1])
                found.append((n, ub, ib))
            terms = []
            for n, ub, ib in found:
                hi, lo = residuals[k][n, :block], residuals[k][n, block:]
                v_hi, v_lo = item_parts[k][ib, :block], item_parts[k][ib, block:]
                terms.append(user_rate * dot_split(hi, lo, v_hi, v_lo))
            for (n, ub, ib), term in zip(found, terms):
                users_next[ub] += term

        over_groups(count, body)
    if step + 1 == sh.steps:
        copy = pltpu.make_async_copy(users_next, users_out, sem)
        copy.start()
    copy.wait()


def whole_in(space):
    return pl.BlockSpec(memory_space=space)


def in_vmem(x):
    return pltpu.with_memory_space_constraint(x, pltpu.VMEM)


def in_smem(x):
    return pltpu.with_memory_space_constraint(x, pltpu.SMEM)


def in_hbm(x):
    return pltpu.with_memory_space_constraint(x, pltpu.HBM)


def params():
    return pltpu.CompilerParams(vmem_limit_bytes=16 << 20)


def load(sh, index, count, users, blocks):
    return pl.pallas_call(
        functools.partial(load_kernel, sh),
        out_shape=[
            pltpu.VMEM(users.shape, users.dtype),
            pltpu.VMEM((sh.total, sh.block, sh.block), blocks.dtype),
            pltpu.SMEM((sh.steps * sh.chunks, sh.total + 1), jnp.int32),
        ],
        in_specs=[whole_in(pltpu.SMEM)] * 2 + [whole_in(pl.ANY)] * 2,
        out_specs=[whole_in(pltpu.VMEM)] * 2 + [whole_in(pltpu.SMEM)],
        scratch_shapes=[pltpu.SemaphoreType.DMA((2,))],
        compiler_params=params(),
    )(*[in_hbm(x) for x in (index, count, users, blocks)])


def item_terms(sh, row, lists, users, ratings, items):
    nu = len(items)
    spec = whole_in(pltpu.VMEM)
    padded = -(-sh.total // GROUPS[0]) * GROUPS[0]
    outs = pl.pallas_call(
        functools.partial(item_kernel, sh, nu, row),
        out_shape=[pltpu.VMEM((sh.block, sh.rank), jnp.float32)] * nu
        + [
            pltpu.VMEM((padded, 2 * sh.block, sh.block), jnp.bfloat16),
            pltpu.VMEM((nu, 2 * sh.block, sh.rank), jnp.bfloat16),
        ],
        in_specs=[whole_in(pltpu.SMEM)] + [spec] * (2 + nu),
        out_specs=[spec] * (2 + nu),
        scratch_shapes=[
            pltpu.VMEM((nu, sh.block, sh.rank), jnp.float32),
            pltpu.VMEM((nu, sh.rank, 2 * sh.block), jnp.bfloat16),
        ],
        compiler_params=params(),
        cost_estimate=pl.CostEstimate(
            flops=sh.total * 8 * sh.block * sh.block * sh.rank // sh.chunks,
            bytes_accessed=8 * sh.total * sh.block * sh.block // sh.chunks,
            transcendentals=0,
        ),
    )(in_smem(lists), *[in_vmem(x) for x in (users, ratings, *items)])
    return outs[:nu], outs[nu], outs[nu + 1]


def new_users(sh, step, lists, users, residuals, item_parts, blocks):
    spec = whole_in(pltpu.VMEM)
    more = step + 1 < sh.steps
    work = sh.total * 8 * sh.block * sh.block * sh.rank
    size = sh.block * sh.block
    if more:
        out_shape = [
            pltpu.VMEM(users.shape, users.dtype),
            pltpu.VMEM((sh.total, sh.block, sh.block), blocks.dtype),
        ]
        out_specs = [spec, spec]
        scratch = []
    else:
        out_shape = [jax.ShapeDtypeStruct(users.shape, users.dtype)]
        out_specs = [whole_in(pl.ANY)]
        scratch = [pltpu.VMEM(users.shape, users.dtype)]
    out = pl.pallas_call(
        functools.partial(user_kernel, sh, step),
        out_shape=out_shape,
        in_specs=[whole_in(pltpu.SMEM)]
        + [spec] * (1 + 2 * sh.chunks)
        + [whole_in(pl.ANY)] * more,
        out_specs=out_specs,
        scratch_shapes=scratch + [pltpu.SemaphoreType.DMA],
        compiler_params=params(),
        cost_estimate=pl.CostEstimate(
            flops=work, bytes_accessed=8 * users.size + 8 * sh.total * size, transcendentals=0
        ),
    )(
        in_smem(lists),
        *[in_vmem(x) for x in (users, *residuals, *item_parts)],
        *[in_hbm(blocks)] * more,
    )
    return out[0], out[1] if more else None


def local(nb, nu, user_factors, item_factors, block_index, block_count, ratings):
    sh = Shape(user_factors, item_factors, block_index, ratings)
    index = block_index.transpose(0, 2, 3, 1)
    count = block_count.transpose(0, 2, 1)
    users = user_factors.reshape(-1, sh.block, sh.rank)
    blocks = ratings.reshape(-1, sh.block, sh.block)
    own = [item_factors[k * sh.block : (k + 1) * sh.block] for k in range(sh.chunks)]
    users, step_ratings, lists = load(sh, index, count, users, blocks)
    for s in range(sh.steps):
        sent, residuals, item_parts = [], [], []
        for k in range(sh.chunks):
            items = [moved(own[k], 0, r, nb, nu) if r else own[k] for r in range(nu)]
            terms, residual, parts = item_terms(
                sh, s * sh.chunks + k, lists, users, step_ratings, items
            )
            residuals.append(residual)
            item_parts.append(parts)
            sent.append([moved(terms[r], 1, r, nb, nu) for r in reversed(range(nu))])
        own = [functools.reduce(jnp.add, x) for x in sent[:-1]]
        own, residuals = lax.optimization_barrier((own, residuals))
        users, step_ratings = new_users(
            sh, s, lists, users, residuals, item_parts, blocks
        )
        sent, users = lax.optimization_barrier((sent[-1], users))
        own.append(functools.reduce(jnp.add, sent))
    return (users.reshape(user_factors.shape), jnp.concatenate(own, axis=0))


def solution(mesh):
    in_specs = (
        P(("blk", "user"), None),
        P(("blk", "user"), None),
        P(None, ("blk", "user"), None, None),
        P(None, ("blk", "user"), None),
        P(None, ("blk", "user"), None, None, None, None),
    )
    out_specs = (P(("blk", "user"), None), P(("blk", "user"), None))
    return jax.shard_map(
        functools.partial(local, mesh.shape["blk"], mesh.shape["user"]),
        mesh=mesh,
        in_specs=in_specs,
        out_specs=out_specs,
        check_vma=False,
    )
```

```python
import functools

import jax
import jax.numpy as jnp
from jax import lax
from jax.experimental import pallas as pl
from jax.experimental.pallas import tpu as pltpu
from jax.sharding import PartitionSpec as P

user_rate = 0.01
item_rate = 0.0015
decay_rate = 0.05
GROUPS = (8, 4)


def divided(x, n):
    return x >> (n.bit_length() - 1) if n & (n - 1) == 0 else lax.div(x, n)


def left_over(x, n):
    return x & (n - 1) if n & (n - 1) == 0 else lax.rem(x, n)


def partner(u, r, n):
    return u ^ r if n & (n - 1) == 0 else (u + r) % n


def source(u, r, n):
    return u ^ r if n & (n - 1) == 0 else (u - r + n) % n


def moved(x, step, r, nb, nu):
    route = [
        (b * nu + u, ((b + step) % nb) * nu + partner(u, r, nu))
        for b in range(nb)
        for u in range(nu)
    ]
    return lax.ppermute(x, ("blk", "user"), route)


def sum_order(nu):
    return [nu - 1, *range(1, nu - 1), 0]


def gather_order(nu):
    return [*range(1, nu), 0]


def split(x):
    hi = x.astype(jnp.bfloat16)
    return hi, (x - hi.astype(jnp.float32)).astype(jnp.bfloat16)


def dot(a, b):
    return jnp.dot(a, b, preferred_element_type=jnp.float32)


def dot_rows(a, b):
    return lax.dot_general(a, b, (((1,), (1,)), ((), ())), preferred_element_type=jnp.float32)


def dot_split(x_hi, x_lo, y_hi, y_lo):
    wide = jnp.concatenate([x_hi, x_lo], axis=1)
    return dot(wide, jnp.concatenate([y_hi, y_hi], axis=0)) + dot(x_hi, y_lo)


def over_groups(count, body):
    first = 0
    for i, size in enumerate(GROUPS):
        groups = divided(count - first + (size - 1 if i + 1 == len(GROUPS) else 0), size)

        def step(g, carry, first=first, size=size):
            body(first + g * size, size)
            return carry

        lax.fori_loop(0, groups, step, 0)
        first = first + groups * size


class Shape:
    def __init__(self, user_factors, item_factors, block_index, ratings):
        self.steps, self.tile_rows, self.tile_cols, self.slots = block_index.shape
        self.block = ratings.shape[-1]
        self.rank = user_factors.shape[1]
        self.parts = user_factors.shape[0] // (self.tile_rows * self.block)
        self.chunks = item_factors.shape[0] // self.block
        self.total = self.tile_rows * self.tile_cols * self.slots
        self.user_blocks = self.tile_rows * self.parts

    def entry(self, packed):
        q = left_over(packed, self.parts * self.parts)
        slot = divided(packed, self.parts * self.parts)
        tile = divided(slot, self.slots)
        row = divided(tile, self.tile_cols) * self.parts + divided(q, self.parts)
        col = left_over(tile, self.tile_cols) * self.parts + left_over(q, self.parts)
        return slot, row, divided(col, self.chunks)


def load_kernel(sh, index_ref, count_ref, users_in, ratings_in, users, ratings, lists, sems):
    copies = [
        pltpu.make_async_copy(users_in, users, sems.at[0]),
        pltpu.make_async_copy(ratings_in.at[pl.ds(0, sh.total)], ratings, sems.at[1]),
    ]
    for copy in copies:
        copy.start()
    for s in range(sh.steps):

        def tile_row(t, found):
            for c in range(sh.tile_cols):
                count = count_ref[s, c, t]
                for k in range(sh.slots):
                    q = index_ref[s, c, k, t]
                    chunk = left_over(q + c * sh.parts, sh.chunks)
                    n = found[0]
                    for j in range(1, sh.chunks):
                        n = jnp.where(chunk == j, found[j], n)
                    slot = (t * sh.tile_cols + c) * sh.slots + k
                    lists[s * sh.chunks + chunk, n + 1] = slot * (sh.parts * sh.parts) + q
                    more = jnp.where(k < count, 1, 0)
                    found = tuple(
                        found[j] + jnp.where(chunk == j, more, 0) for j in range(sh.chunks)
                    )
            return found

        found = lax.fori_loop(0, sh.tile_rows, tile_row, (jnp.int32(0),) * sh.chunks)
        for j in range(sh.chunks):
            lists[s * sh.chunks + j, 0] = found[j]
    for copy in copies:
        copy.wait()


def item_kernel(sh, nu, row, *refs):
    list_ref, users, ratings = refs[:3]
    items = dict(zip(gather_order(nu), refs[3 : 3 + nu]))
    terms = refs[3 + nu : 3 + 2 * nu]
    residuals, item_parts, grads, item_turned = refs[3 + 2 * nu :]
    block = sh.block
    me = lax.axis_index("user")
    for r in range(nu):
        hi, lo = split(items[r][...])
        at = source(me, r, nu)
        item_parts[at, :block] = hi
        item_parts[at, block:] = lo
        hi, lo = split(items[r][...].T)
        item_turned[at, :, :block] = hi
        item_turned[at, :, block:] = lo
    grads[...] = jnp.zeros_like(grads)
    count = list_ref[row, 0]

    def body(first, size):
        found = []
        for n in [first + j for j in range(size)]:
            slot, ub, ib = sh.entry(list_ref[row, jnp.minimum(n, count - 1) + 1])
            found.append((n, slot, ub, ib, jnp.where(n < count, 0, 1 << 30)))
        predicted = []
        for n, slot, ub, ib, least in found:
            u_hi, u_lo = split(users[ub])
            wide = dot(u_hi, item_turned[ib])
            narrow = dot(u_lo, item_turned[ib, :, :block])
            predicted.append((wide[:, block:] + narrow) + wide[:, :block])
        kept = []
        for (n, slot, ub, ib, least), p in zip(found, predicted):
            rating = ratings[slot]
            kept.append(jnp.where(rating > least, 0.5 * rating.astype(jnp.float32) - p, 0.0))
        sums = [
            dot_split(*split(residual.T), *split(users[ub]))
            for (n, slot, ub, ib, least), residual in zip(found, kept)
        ]
        for (n, slot, ub, ib, least), term in zip(found, sums):
            grads[ib] += term
        for (n, slot, ub, ib, least), residual in zip(found, kept):
            hi, lo = split(residual)
            residuals[n, :block] = hi
            residuals[n, block:] = lo

    over_groups(count, body)
    for r in range(nu):
        term = item_rate * grads[partner(me, r, nu)]
        if r == 0:
            term += items[0][...] * (1.0 - item_rate * decay_rate)
        terms[r][...] = term


def user_kernel(sh, step, *refs):
    list_ref, users = refs[:2]
    residuals = refs[2 : 2 + sh.chunks]
    item_parts = refs[2 + sh.chunks : 2 + 2 * sh.chunks]
    row = step * sh.chunks
    if step + 1 < sh.steps:
        ratings_in, users_next, ratings, sem = refs[2 + 2 * sh.chunks :]
        copy = pltpu.make_async_copy(
            ratings_in.at[pl.ds((step + 1) * sh.total, sh.total)], ratings, sem
        )
        copy.start()
    else:
        users_out, users_next, sem = refs[2 + 2 * sh.chunks :]
    block = sh.block

    def scale(i, carry):
        users_next[i] = users[i] * (1.0 - user_rate * decay_rate)
        return carry

    lax.fori_loop(0, sh.user_blocks, scale, 0)
    for k in range(sh.chunks):
        count = list_ref[row + k, 0]

        def body(first, size, k=k, count=count):
            found = []
            for n in [first + j for j in range(size)]:
                slot, ub, ib = sh.entry(list_ref[row + k, jnp.minimum(n, count - 1) + 1])
                found.append((n, ub, ib))
            terms = []
            for n, ub, ib in found:
                hi, lo = residuals[k][n, :block], residuals[k][n, block:]
                v_hi, v_lo = item_parts[k][ib, :block], item_parts[k][ib, block:]
                terms.append(user_rate * dot_split(hi, lo, v_hi, v_lo))
            for (n, ub, ib), term in zip(found, terms):
                users_next[ub] += term

        over_groups(count, body)
    if step + 1 == sh.steps:
        copy = pltpu.make_async_copy(users_next, users_out, sem)
        copy.start()
    copy.wait()


def whole_in(space):
    return pl.BlockSpec(memory_space=space)


def in_vmem(x):
    return pltpu.with_memory_space_constraint(x, pltpu.VMEM)


def in_smem(x):
    return pltpu.with_memory_space_constraint(x, pltpu.SMEM)


def in_hbm(x):
    return pltpu.with_memory_space_constraint(x, pltpu.HBM)


def params():
    return pltpu.CompilerParams(vmem_limit_bytes=16 << 20)


def load(sh, index, count, users, blocks):
    return pl.pallas_call(
        functools.partial(load_kernel, sh),
        out_shape=[
            pltpu.VMEM(users.shape, users.dtype),
            pltpu.VMEM((sh.total, sh.block, sh.block), blocks.dtype),
            pltpu.SMEM((sh.steps * sh.chunks, sh.total + 1), jnp.int32),
        ],
        in_specs=[whole_in(pltpu.SMEM)] * 2 + [whole_in(pl.ANY)] * 2,
        out_specs=[whole_in(pltpu.VMEM)] * 2 + [whole_in(pltpu.SMEM)],
        scratch_shapes=[pltpu.SemaphoreType.DMA((2,))],
        compiler_params=params(),
    )(*[in_hbm(x) for x in (index, count, users, blocks)])


def item_terms(sh, row, lists, users, ratings, items):
    nu = len(items)
    spec = whole_in(pltpu.VMEM)
    padded = -(-sh.total // GROUPS[0]) * GROUPS[0]
    outs = pl.pallas_call(
        functools.partial(item_kernel, sh, nu, row),
        out_shape=[pltpu.VMEM((sh.block, sh.rank), jnp.float32)] * nu
        + [
            pltpu.VMEM((padded, 2 * sh.block, sh.block), jnp.bfloat16),
            pltpu.VMEM((nu, 2 * sh.block, sh.rank), jnp.bfloat16),
        ],
        in_specs=[whole_in(pltpu.SMEM)] + [spec] * (2 + nu),
        out_specs=[spec] * (2 + nu),
        scratch_shapes=[
            pltpu.VMEM((nu, sh.block, sh.rank), jnp.float32),
            pltpu.VMEM((nu, sh.rank, 2 * sh.block), jnp.bfloat16),
        ],
        compiler_params=params(),
        cost_estimate=pl.CostEstimate(
            flops=sh.total * 8 * sh.block * sh.block * sh.rank // sh.chunks,
            bytes_accessed=8 * sh.total * sh.block * sh.block // sh.chunks,
            transcendentals=0,
        ),
    )(in_smem(lists), *[in_vmem(x) for x in (users, ratings, *[items[r] for r in gather_order(nu)])])
    return outs[:nu], outs[nu], outs[nu + 1]


def new_users(sh, step, lists, users, residuals, item_parts, blocks):
    spec = whole_in(pltpu.VMEM)
    more = step + 1 < sh.steps
    work = sh.total * 8 * sh.block * sh.block * sh.rank
    size = sh.block * sh.block
    if more:
        out_shape = [
            pltpu.VMEM(users.shape, users.dtype),
            pltpu.VMEM((sh.total, sh.block, sh.block), blocks.dtype),
        ]
        out_specs = [spec, spec]
        scratch = []
    else:
        out_shape = [jax.ShapeDtypeStruct(users.shape, users.dtype)]
        out_specs = [whole_in(pl.ANY)]
        scratch = [pltpu.VMEM(users.shape, users.dtype)]
    out = pl.pallas_call(
        functools.partial(user_kernel, sh, step),
        out_shape=out_shape,
        in_specs=[whole_in(pltpu.SMEM)]
        + [spec] * (1 + 2 * sh.chunks)
        + [whole_in(pl.ANY)] * more,
        out_specs=out_specs,
        scratch_shapes=scratch + [pltpu.SemaphoreType.DMA],
        compiler_params=params(),
        cost_estimate=pl.CostEstimate(
            flops=work, bytes_accessed=8 * users.size + 8 * sh.total * size, transcendentals=0
        ),
    )(
        in_smem(lists),
        *[in_vmem(x) for x in (users, *residuals, *item_parts)],
        *[in_hbm(blocks)] * more,
    )
    return out[0], out[1] if more else None


def local(nb, nu, user_factors, item_factors, block_index, block_count, ratings):
    sh = Shape(user_factors, item_factors, block_index, ratings)
    index = block_index.transpose(0, 2, 3, 1)
    count = block_count.transpose(0, 2, 1)
    users = user_factors.reshape(-1, sh.block, sh.rank)
    blocks = ratings.reshape(-1, sh.block, sh.block)
    own = [item_factors[k * sh.block : (k + 1) * sh.block] for k in range(sh.chunks)]
    users, step_ratings, lists = load(sh, index, count, users, blocks)
    for s in range(sh.steps):
        sent, residuals, item_parts = [], [], []
        for k in range(sh.chunks):
            items = [moved(own[k], 0, r, nb, nu) if r else own[k] for r in range(nu)]
            terms, residual, parts = item_terms(
                sh, s * sh.chunks + k, lists, users, step_ratings, items
            )
            residuals.append(residual)
            item_parts.append(parts)
            sent.append([moved(terms[r], 1, r, nb, nu) for r in sum_order(nu)])
        own = [functools.reduce(jnp.add, x) for x in sent[:-1]]
        own, residuals = lax.optimization_barrier((own, residuals))
        users, step_ratings = new_users(
            sh, s, lists, users, residuals, item_parts, blocks
        )
        sent, users = lax.optimization_barrier((sent[-1], users))
        own.append(functools.reduce(jnp.add, sent))
    return (users.reshape(user_factors.shape), jnp.concatenate(own, axis=0))


def solution(mesh):
    in_specs = (
        P(("blk", "user"), None),
        P(("blk", "user"), None),
        P(None, ("blk", "user"), None, None),
        P(None, ("blk", "user"), None),
        P(None, ("blk", "user"), None, None, None, None),
    )
    out_specs = (P(("blk", "user"), None), P(("blk", "user"), None))
    return jax.shard_map(
        functools.partial(local, mesh.shape["blk"], mesh.shape["user"]),
        mesh=mesh,
        in_specs=in_specs,
        out_specs=out_specs,
        check_vma=False,
    )
```
